32 devices in a mesh: groups: 2 (over y), xfer: 4 (over x, core), tensor: 4 (over z).
Axes of the slice: x: 2, y: 2, z: 4, core: 2. Of those that a mesh axis runs over, the one named last changes fastest.
Arguments:
- kv_values: bfloat16 [131072, 576], P(('groups', 'xfer', 'tensor')), parts along dimension 0, may hold values from -8 to 8
- kv_scales: bfloat16 [131072, 4], P(('groups', 'xfer', 'tensor')), parts along dimension 0, may hold values from 0.29882812 to 3
- decode_of: int32 [256], P('groups'), parts along dimension 0, may hold values from 0 to 3, as said below
- kv_lengths: int32 [256], P('groups'), parts along dimension 0, may hold values from 1 to 512, as said below
- q_nope: bfloat16 [256, 4, 16384], P(('groups', 'xfer'), None, 'tensor'), parts along dimension 0, may hold values from -6 to 6
- q_rope: bfloat16 [256, 4, 8192], P(('groups', 'xfer'), None, 'tensor'), parts along dimension 0, may hold values from -8 to 8
- new_kv: bfloat16 [256, 4, 576], P(('groups', 'xfer')), parts along dimension 0, may hold values from -6 to 6
- wk_up: bfloat16 [128, 128, 512], P('tensor'), may hold values from -0.5 to 0.5
- wv_up: bfloat16 [128, 512, 128], P('tensor'), may hold values from -0.25 to 0.25
- w_out: bfloat16 [16384, 3584], P('tensor'), may hold values from -0.046875 to 0.046875
Outputs:
- attn_output: bfloat16 [256, 4, 3584], P(('groups', 'xfer', 'tensor')), parts along dimension 0
The draws below stay inside these ranges and needn't reach their ends.
There are 2 independent parts, one for each index of `groups`. The reference program is written for one: setup_inputs(seed, part) draws one part's arguments, and reference() takes and returns one part's arrays. A program takes and returns all parts, laid end to end along the dimension named above; an argument that names none is the same for every part. Nothing has to cross between parts.
Inputs may be any that keep to these rules, and one draw needn't show every extreme that they name: `decode_of`: requests i * 32 to (i + 1) * 32 - 1 were prefilled by group i. Every decode group is named by exactly 32 requests. From each prefill group 8 requests go to each decode group, except for two crossed pairs of prefill and decode groups: two pairs carry 12 requests and the two opposite pairs 8 - 4. `kv_lengths`: some request has length 512.
All inputs are finite; a program needn't handle non-finite values.
Results may differ from the reference program's by a relative error of at most 0.012.
Values may be sent and summed in bfloat16 or wider, within the bound.
No kernel may reach another device: no remote copies, remote signals or barrier semaphores. Data moves between devices by JAX's collectives and lax.ppermute only.
A program may use at most 192 MiB of HBM per device.

```python
import math
import jax
import jax.numpy as jnp
from jax import lax

H = 128
DC = 512
DR = 64
DN = 128
DV = 128
DOUT = 3584
NB = 4
REQ_DEV = 32
LMAX = 512
STEPS = 4
REQS = 128
SPAN = 128
N_XFER = 4
N_TENSOR = 4


def draw_kv_values(key, part):
    key = jax.random.fold_in(key, 3)
    first_key, second_key = jax.random.split(key)
    row_total = REQS * LMAX
    latent = jnp.clip(jax.random.normal(first_key, (row_total, DC)), -6.0, 6.0)
    rope_part = jnp.clip(jax.random.normal(second_key, (row_total, DR)), -6.0, 6.0)
    return jnp.concatenate([latent, rope_part], axis=1).astype(jnp.bfloat16)


def draw_q_rope(key, part):
    key = jax.random.fold_in(key, 5)
    first_key = jax.random.fold_in(key, 0)
    full_shape = (REQS, STEPS, H, DR)
    values = jnp.clip(jax.random.normal(first_key, full_shape), -6.0, 6.0)
    return values.reshape(REQS, STEPS, H * DR).astype(jnp.bfloat16)


def draw_kv_lengths(key, part):
    key = jax.random.fold_in(key, 7)
    first_key, second_key = jax.random.split(key)
    lengths = jax.random.randint(first_key, (REQS,), 1, LMAX + 1)
    longest = jax.random.randint(second_key, (), 0, REQS)
    return jnp.where(jnp.arange(REQS) == longest, LMAX, lengths).astype(jnp.int32)


def draw_decode_of(key, part):
    key = jax.random.fold_in(key, 11)
    groups = REQS // REQ_DEV
    pair_share = REQ_DEV // groups
    extra_load = pair_share // 2
    key_one, key_two, key_three, key_four, key_five = jax.random.split(key, 5)
    first_src = jax.random.randint(key_one, (), 0, groups)
    second_src = (first_src + jax.random.randint(key_two, (), 1, groups)) % groups
    first_dst = jax.random.randint(key_three, (), 0, groups)
    second_dst = (first_dst + jax.random.randint(key_four, (), 1, groups)) % groups
    src_grid = jnp.arange(groups)[:, None]
    dst_grid = jnp.arange(groups)[None, :]
    gain_one = ((src_grid == first_src) & (dst_grid == first_dst)).astype(jnp.int32)
    loss_one = ((src_grid == first_src) & (dst_grid == second_dst)).astype(jnp.int32)
    loss_two = ((src_grid == second_src) & (dst_grid == first_dst)).astype(jnp.int32)
    gain_two = ((src_grid == second_src) & (dst_grid == second_dst)).astype(jnp.int32)
    counts = pair_share + extra_load * (gain_one + gain_two - loss_one - loss_two)
    bounds = jnp.cumsum(counts, axis=1)
    position = jnp.arange(REQ_DEV)
    labels = jnp.sum((position[None, :, None] >= bounds[:, None, :]).astype(jnp.int32), axis=2)
    group_keys = jax.random.split(key_five, groups)
    shuffles = jax.vmap(lambda group_key: jax.random.permutation(group_key, REQ_DEV))(group_keys)
    labels = jnp.take_along_axis(labels, shuffles, axis=1)
    return labels.reshape(-1).astype(jnp.int32)


def level_of(stream_key, shape, cuts, least, largest):
    def one(dim, blocks):
        steps = jax.random.uniform(jax.random.fold_in(jax.random.fold_in(stream_key, 6), dim), (blocks,), jnp.float32, least / len(cuts), largest / len(cuts))
        return jnp.repeat(jnp.exp(steps), shape[dim] // blocks).reshape((-1,) + (1,) * (len(shape) - dim - 1))

    level = one(*cuts[0])
    for cut in cuts[1:]:
        level = level * one(*cut)
    return level


def noise(own_key, dims, deviation, reach, shards=(), held_as=jnp.bfloat16):
    array = jax.random.normal(own_key, dims, jnp.float32) * deviation
    if len(shards) > 0:
        array = level_of(own_key, dims, shards, -0.22, 0.18) * array
    return jnp.clip(array, min=-reach, max=reach).astype(held_as)


def setup_inputs(seed: int = 0, part: int = 0) -> dict:
    key_list = jax.random.split(jax.random.key(seed), 11)
    part_splits = jax.random.split(jax.random.fold_in(key_list[10], part), 11)
    return {
        "kv_values": draw_kv_values(jax.random.fold_in(jax.random.fold_in(key_list[10], part), 71), part),
        "kv_scales": jnp.clip(jnp.exp(math.log(3.0) - 2.306499 * jax.random.uniform(part_splits[1], (REQS * LMAX, NB), jnp.float32) ** level_of(part_splits[1], (REQS * LMAX, NB), ((0, 16),), -0.2, 0.2)), 0.29882812, 3.0).astype(jnp.bfloat16),
        "decode_of": draw_decode_of(jax.random.fold_in(jax.random.fold_in(key_list[10], part), 71), part),
        "kv_lengths": draw_kv_lengths(jax.random.fold_in(jax.random.fold_in(key_list[10], part), 71), part),
        "q_nope": noise(part_splits[4], (REQS, STEPS, H * DN), 1.0, 6.0, ((0, 4), (2, 4))),
        "q_rope": draw_q_rope(jax.random.fold_in(jax.random.fold_in(key_list[10], part), 71), part),
        "new_kv": noise(part_splits[6], (REQS, STEPS, DC + DR), 1.0, 6.0, ((0, 4),)),
        "wk_up": noise(key_list[7], (H, DN, DC), DN ** -0.5, 0.5, ((0, 4),)),
        "wv_up": noise(key_list[8], (H, DC, DV), DC ** -0.5, 0.25, ((0, 4),)),
        "w_out": noise(key_list[9], (H * DV, DOUT), (H * DV) ** -0.5, 0.046875, ((0, 4),)),
    }


def dequantize(values, scales):
    latent = values[..., :DC].astype(jnp.float32)
    leading = latent.shape[:-1]
    blocks = scales.shape[-1]
    latent = latent.reshape(leading + (blocks, DC // blocks)) * scales.astype(jnp.float32)[..., None]
    latent = latent.reshape(leading + (DC,)).astype(jnp.bfloat16)
    return jnp.concatenate([latent, values[..., DC:]], axis=-1)

def reference(kv_values, kv_scales, decode_of, kv_lengths, q_nope, q_rope, new_kv, wk_up, wv_up, w_out):
    row_width = DC + DR
    kv_cache = dequantize(kv_values, kv_scales)
    kv_cache = kv_cache.reshape(N_XFER, N_TENSOR, REQ_DEV, SPAN, row_width)
    kv_cache = kv_cache.transpose(0, 2, 1, 3, 4).reshape(REQS, LMAX, row_width)
    slot_order = jnp.argsort(decode_of, stable=True).astype(jnp.int32)
    score_scale = 1.0 / math.sqrt(DN + DR)
    query_heads = q_nope.reshape(REQS, STEPS, H, DN).astype(jnp.float32)
    query_latent = jnp.einsum('sthn,hnc->sthc', query_heads, wk_up.astype(jnp.float32)).astype(jnp.bfloat16)
    queries = jnp.concatenate([query_latent, q_rope.reshape(REQS, STEPS, H, DR)], axis=-1)
    position = jnp.arange(LMAX, dtype=jnp.int32)
    step_ids = jnp.arange(STEPS, dtype=jnp.int32)
    causal = step_ids[None, :] <= step_ids[:, None]

    def attend(slot_index):
        request = slot_order[slot_index]
        key_rows = jnp.concatenate([kv_cache[request], new_kv[slot_index]], axis=0)
        own_queries = queries[slot_index]
        scores = jnp.einsum('thc,kc->thk', own_queries.astype(jnp.float32), key_rows.astype(jnp.float32)) * score_scale
        live_cache = jnp.broadcast_to((position < kv_lengths[request])[None, :], (STEPS, LMAX))
        live_mask = jnp.concatenate([live_cache, causal], axis=1)
        scores = jnp.where(live_mask[:, None, :], scores, -jnp.inf)
        row_max = lax.optimization_barrier(jnp.max(scores, axis=-1, keepdims=True))
        exp_weights = jnp.exp(scores - row_max)
        weight_sum = lax.optimization_barrier(jnp.sum(exp_weights, axis=-1))
        weights = exp_weights.astype(jnp.bfloat16)
        mixed = jnp.einsum('thk,kc->thc', weights.astype(jnp.float32), key_rows[:, :DC].astype(jnp.float32))
        return (mixed / weight_sum[..., None]).astype(jnp.bfloat16)
    latents = lax.map(attend, jnp.arange(REQS, dtype=jnp.int32))
    head_out = jnp.einsum('sthc,hcv->sthv', latents.astype(jnp.float32), wv_up.astype(jnp.float32)).astype(jnp.bfloat16)
    flat_heads = head_out.reshape(REQS * STEPS, H * DV)
    projected = jnp.dot(flat_heads, w_out, preferred_element_type=jnp.float32).astype(jnp.bfloat16)
    return projected.reshape(REQS, STEPS, DOUT)
```

```python
import math

import jax
import jax.numpy as jnp
from jax import lax
from jax.experimental import pallas as pl
from jax.experimental.pallas import tpu as pltpu
from jax.sharding import PartitionSpec as P

MASKED_SCORE = -1e30
NEW_ROWS = 16


SHORT = pl.CostEstimate(flops=1024, bytes_accessed=1024, transcendentals=0)


def pack_kernel(groups, blocks, index_ref, *refs):
    values, scales = refs[:groups], refs[groups : 2 * groups]
    outs = refs[len(refs) - groups :]
    for value_ref, scale_ref, out_ref in zip(values, scales, outs):
        width = value_ref.shape[-2]
        latent_width = blocks * 128
        span = value_ref.shape[-1]
        factor = scale_ref[...].reshape(blocks, span).astype(jnp.float32)
        for block in range(blocks):
            rows = slice(block * 128, (block + 1) * 128)
            part = value_ref[..., rows, :].reshape(128, span).astype(jnp.float32)
            out_ref[0, rows, :] = (part * factor[block : block + 1, :]).astype(jnp.bfloat16)
        rest = value_ref[..., latent_width:width, :]
        out_ref[0, latent_width:width, :] = rest.reshape(width - latent_width, span)


def pack(values, scales, index, span, waits=()):
    groups, count = index.shape
    width, blocks = values.shape[-2], scales.shape[-2]

    def spec(rows, group):
        if values.ndim == 2:
            return pl.BlockSpec((rows, span), lambda n, index_ref: (0, index_ref[group, n]))
        return pl.BlockSpec((1, rows, span), lambda n, index_ref: (index_ref[group, n], 0, 0))

    return pl.pallas_call(
        lambda *refs: pack_kernel(groups, blocks, *refs),
        grid_spec=pltpu.PrefetchScalarGridSpec(
            num_scalar_prefetch=1,
            grid=(count,),
            in_specs=[spec(width, g) for g in range(groups)]
            + [spec(blocks, g) for g in range(groups)]
            + [pl.BlockSpec(memory_space=pl.ANY)] * len(waits),
            out_specs=[pl.BlockSpec((1, width, span), lambda n, index_ref: (n, 0, 0))] * groups,
        ),
        out_shape=[jax.ShapeDtypeStruct((count, width, span), jnp.bfloat16)] * groups,
        cost_estimate=SHORT,
    )(index, *([values] * groups), *([scales] * groups), *waits)


def pack_all(values, scales, index, span, *waits):
    groups, count = index.shape
    width, blocks = values.shape[-2], scales.shape[-2]

    def kernel(index_ref, *refs):
        outs = [refs[-1].at[g] for g in range(groups)]
        pack_kernel(groups, blocks, index_ref, *refs[: 2 * groups], *outs)

    def spec(rows, group):
        if values.ndim == 2:
            return pl.BlockSpec((rows, span), lambda n, index_ref: (0, index_ref[group, n]))
        return pl.BlockSpec((1, rows, span), lambda n, index_ref: (index_ref[group, n], 0, 0))

    return pl.pallas_call(
        kernel,
        grid_spec=pltpu.PrefetchScalarGridSpec(
            num_scalar_prefetch=1,
            grid=(count,),
            in_specs=[spec(width, g) for g in range(groups)]
            + [spec(blocks, g) for g in range(groups)]
            + [pl.BlockSpec(memory_space=pl.ANY)] * len(waits),
            out_specs=pl.BlockSpec(
                (groups, 1, width, span), lambda n, index_ref: (0, n, 0, 0)
            ),
        ),
        out_shape=jax.ShapeDtypeStruct((groups, count, width, span), jnp.bfloat16),
        cost_estimate=SHORT,
    )(index, *([values] * groups), *([scales] * groups), *waits)


def held(x, *waits):
    def kernel(*refs):
        pass

    anywhere = pl.BlockSpec(memory_space=pl.ANY)
    return pl.pallas_call(
        kernel,
        in_specs=[anywhere] * (1 + len(waits)),
        out_specs=anywhere,
        out_shape=jax.ShapeDtypeStruct(x.shape, x.dtype),
        input_output_aliases={0: 0},
    )(x, *waits)


def regroup_kernel(count, *refs):
    refs = refs[: 2 * count] + refs[-2:]
    for k in range(count):
        refs[2 * count][k, 0] = refs[k][0]
        refs[2 * count + 1][k, 0] = refs[count + k][0]


def regroup(landed, *waits):
    count, (rows, width, span) = len(landed), landed[0].shape
    half = rows // 2
    own = pl.BlockSpec((1, width, span), lambda n: (n, 0, 0))
    far = pl.BlockSpec((1, width, span), lambda n: (half + n, 0, 0))
    outs = pl.pallas_call(
        lambda *refs: regroup_kernel(count, *refs),
        grid=(half,),
        in_specs=[own] * count
        + [far] * count
        + [pl.BlockSpec(memory_space=pl.ANY)] * len(waits),
        out_specs=[pl.BlockSpec((count, 1, width, span), lambda n: (0, n, 0, 0))] * 2,
        out_shape=[jax.ShapeDtypeStruct((count, half, width, span), jnp.bfloat16)] * 2,
        cost_estimate=SHORT,
    )(*landed, *landed, *waits)
    return tuple(x.reshape(count * half, width, span) for x in outs)


def select_kernel(which_ref, index_ref, *refs):
    n = pl.program_id(0)
    sources = (len(refs) - 2) // 2
    for side in range(2):
        for source in range(sources):

            @pl.when(which_ref[side, n] == source)
            def _(side=side, source=source):
                refs[2 * sources + side][...] = refs[side * sources + source][...]


def select_blocks(arrived, which, index):
    count = index.shape[1]
    width, span = arrived[0].shape[1:]

    def pick(side, source):
        def place(n, which_ref, index_ref):
            return jnp.where(which_ref[side, n] == source, index_ref[side, n], 0), 0, 0

        return pl.BlockSpec((1, width, span), place)

    return pl.pallas_call(
        select_kernel,
        grid_spec=pltpu.PrefetchScalarGridSpec(
            num_scalar_prefetch=2,
            grid=(count,),
            in_specs=[pick(i, j) for i in range(2) for j in range(len(arrived))],
            out_specs=[pl.BlockSpec((1, width, span), lambda n, *refs: (n, 0, 0))] * 2,
        ),
        out_shape=[jax.ShapeDtypeStruct((count, width, span), jnp.bfloat16)] * 2,
        cost_estimate=SHORT,
    )(which, index, *arrived, *arrived)


def in_order(pieces, replica):
    count, shape = len(pieces), pieces[0].shape

    def kernel(replica_ref, *refs):
        out_ref, done = refs[count], refs[count + 1]
        copies = [
            pltpu.make_async_copy(refs[t], out_ref.at[replica_ref[0] ^ t], done.at[t])
            for t in range(count)
        ]
        for copy in copies:
            copy.start()
        for copy in copies:
            copy.wait()

    anywhere = pl.BlockSpec(memory_space=pl.ANY)
    return pl.pallas_call(
        kernel,
        in_specs=[pl.BlockSpec(memory_space=pltpu.SMEM)] + [anywhere] * count,
        out_specs=pl.BlockSpec(memory_space=pltpu.VMEM),
        out_shape=jax.ShapeDtypeStruct((count,) + shape, pieces[0].dtype),
        scratch_shapes=[pltpu.SemaphoreType.DMA((count,))],
        cost_estimate=SHORT,
    )(replica[None], *pieces)


def cut(flat, pieces, which, *waits):
    rows, columns = flat.shape[0] // pieces, flat.shape[1]

    def kernel(which_ref, flat_ref, *refs):
        refs[-1][...] = flat_ref[...]

    return pl.pallas_call(
        kernel,
        grid_spec=pltpu.PrefetchScalarGridSpec(
            num_scalar_prefetch=1,
            grid=(1,),
            in_specs=[pl.BlockSpec((rows, columns), lambda n, which_ref: (which_ref[0], 0))]
            + [pl.BlockSpec(memory_space=pl.ANY)] * len(waits),
            out_specs=pl.BlockSpec((rows, columns), lambda n, which_ref: (0, 0)),
        ),
        out_shape=jax.ShapeDtypeStruct((rows, columns), flat.dtype),
        cost_estimate=SHORT,
    )(which[None], flat, *waits)


def by_side(arrays, index, *waits):
    count = index.shape[1]

    def pick(side, x):
        return pl.BlockSpec(
            (1,) + x.shape[1:], lambda n, index_ref: (index_ref[side, n], 0, 0)
        )

    def kernel(index_ref, *refs):
        for i in range(2 * len(arrays)):
            refs[i - 2 * len(arrays)][...] = refs[i][...]

    return pl.pallas_call(
        kernel,
        grid_spec=pltpu.PrefetchScalarGridSpec(
            num_scalar_prefetch=1,
            grid=(count,),
            in_specs=[pick(side, x) for x in arrays for side in range(2)]
            + [pl.BlockSpec(memory_space=pl.ANY)] * len(waits),
            out_specs=[
                pl.BlockSpec((1,) + x.shape[1:], lambda n, index_ref: (n, 0, 0))
                for x in arrays
                for side in range(2)
            ],
        ),
        out_shape=[
            jax.ShapeDtypeStruct((count,) + x.shape[1:], x.dtype)
            for x in arrays
            for side in range(2)
        ],
        cost_estimate=SHORT,
    )(index, *[x for x in arrays for side in range(2)], *waits)


def attend_kernel(shards, steps, score_scale, scalars, *refs):
    queries = refs[:4]
    keys = refs[4 : 4 + shards]
    new_ref, own_out, other_out = refs[4 + shards], refs[-2], refs[-1]
    own_latent, other_latent, own_rope, other_rope = queries
    latent_width = own_latent.shape[2]
    span = keys[0].shape[2]
    length = scalars[1 + pl.program_id(0)]
    shard = scalars[0]
    key_columns = jnp.concatenate([ref[0] for ref in keys], axis=1)
    new_rows = new_ref[0]
    query = jnp.concatenate([own_latent[0], other_latent[0]], axis=0)
    rope = jnp.concatenate([own_rope[0], other_rope[0]], axis=0)
    across = (((1,), (1,)), ((), ()))
    along = (((1,), (0,)), ((), ()))

    def product(left, right, contract):
        return lax.dot_general(left, right, contract, preferred_element_type=jnp.float32)

    cache_scores = score_scale * (
        product(query, key_columns[:latent_width], along)
        + product(rope, key_columns[latent_width:], along)
    )
    new_scores = score_scale * (
        product(query, new_rows[:, :latent_width], across)
        + product(rope, new_rows[:, latent_width:], across)
    )
    column = lax.broadcasted_iota(jnp.int32, cache_scores.shape, 1)
    position = (shard ^ (column // span)) * span + column % span
    cache_live = position < length
    half = own_latent.shape[1]
    row = lax.broadcasted_iota(jnp.int32, new_scores.shape, 0)
    step = (row % half) // (half // steps)
    new_live = lax.broadcasted_iota(jnp.int32, new_scores.shape, 1) <= step
    cache_scores = jnp.where(cache_live, cache_scores, MASKED_SCORE)
    new_scores = jnp.where(new_live, new_scores, MASKED_SCORE)
    top = jnp.maximum(
        jnp.max(cache_scores, axis=1, keepdims=True), jnp.max(new_scores, axis=1, keepdims=True)
    )
    cache_weights = jnp.where(cache_live, jnp.exp(cache_scores - top), 0.0)
    new_weights = jnp.where(new_live, jnp.exp(new_scores - top), 0.0)
    weight_sum = jnp.sum(cache_weights, axis=1, keepdims=True) + jnp.sum(
        new_weights, axis=1, keepdims=True
    )
    mixed = product(
        cache_weights.astype(jnp.bfloat16), key_columns[:latent_width], across
    ) + product(new_weights.astype(jnp.bfloat16), new_rows[:, :latent_width], along)
    latent = (mixed / weight_sum).astype(jnp.bfloat16)
    own_out[0] = latent[:half]
    other_out[0] = latent[half:]


def attend(scalars, start, queries, keys, new_rows, steps, score_scale, waits):
    count, (half, latent_width) = keys[0].shape[0], queries[0].shape[1:]
    rope_width = queries[2].shape[2]
    width, span = keys[0].shape[1:]
    shards = len(keys)

    def block(rows, columns, first=0):
        return pl.BlockSpec((1, rows, columns), lambda n, scalars: (first + n, 0, 0))

    return pl.pallas_call(
        lambda *refs: attend_kernel(shards, steps, score_scale, *refs),
        grid_spec=pltpu.PrefetchScalarGridSpec(
            num_scalar_prefetch=1,
            grid=(count,),
            in_specs=[block(half, latent_width, start)] * 2
            + [block(half, rope_width, start)] * 2
            + [block(width, span)] * shards
            + [block(NEW_ROWS, width, start)]
            + [pl.BlockSpec(memory_space=pl.ANY)] * len(waits),
            out_specs=[block(half, latent_width)] * 2,
        ),
        out_shape=[jax.ShapeDtypeStruct((count, half, latent_width), jnp.bfloat16)] * 2,
        compiler_params=pltpu.CompilerParams(vmem_limit_bytes=32 * 1024 * 1024),
        cost_estimate=SHORT,
    )(scalars, *queries, *keys, new_rows, *waits)


def local(kv_values, kv_scales, decode_of, kv_lengths, q_nope, q_rope, new_kv, wk_up, wv_up, w_out):
    groups = lax.axis_size("xfer")
    shards = lax.axis_size("tensor")
    me = lax.axis_index("xfer")
    shard = lax.axis_index("tensor")
    parity = shard % 2
    requests = decode_of.shape[0]
    per_group = requests // groups
    row_width = kv_values.shape[1]
    span = kv_values.shape[0] // per_group
    pair_share = per_group // groups
    pair_room = pair_share + pair_share // 2
    sure = pair_share - pair_share // 2
    late = pair_share // 2
    heads_here, nope_width, latent_width = wk_up.shape
    value_width = wv_up.shape[2]
    steps = q_nope.shape[1]
    rope_width = q_rope.shape[2] // heads_here
    score_scale = 1.0 / math.sqrt(nope_width + rope_width)
    out_rows = per_group // shards
    half = per_group // 2
    half_sure = sure // 2
    late_half = (per_group - groups * sure) // 4
    sizes = [2 * half_sure, (groups - 2) * half_sure, late_half, late_half]
    starts = [0, sizes[0], sizes[0] + sizes[1], sizes[0] + sizes[1] + sizes[2]]
    late_start = starts[2]

    def across(x, axis, offset, name="other"):
        with jax.named_scope(f"{name}_{axis if isinstance(axis, str) else 'both'}{offset}"):
            return lax.ppermute(x, axis, [(i, i ^ offset) for i in range(lax.axis_size(axis))])

    dest_here = lax.dynamic_slice_in_dim(decode_of, me * per_group, per_group)
    here = jnp.arange(per_group, dtype=jnp.int32)
    rank_here = jnp.sum(
        ((dest_here[:, None] == dest_here[None, :]) & (here[None, :] < here[:, None])).astype(
            jnp.int32
        ),
        axis=1,
    )
    place_here = dest_here * pair_room + rank_here
    early_ranks = jnp.arange(sure, dtype=jnp.int32)
    early_ranks = (early_ranks + parity * half_sure) % sure
    offsets = jnp.arange(groups, dtype=jnp.int32)
    early_places = (me ^ offsets)[:, None] * pair_room + early_ranks[None, :]
    late_ranks = jnp.arange(late, dtype=jnp.int32)
    middle_places = offsets[:, None] * pair_room + sure + late_ranks[None, :]
    last_places = middle_places + late

    def request_at(places):
        hit = places[..., None] == place_here
        return jnp.sum(jnp.where(hit, here, 0), axis=-1)

    if span % 128 == 0:
        values, scales = kv_values.T, kv_scales.T
    else:
        values = kv_values.reshape(per_group, span, -1).swapaxes(1, 2)
        scales = kv_scales.reshape(per_group, span, -1).swapaxes(1, 2)
    early = pack(values, scales, request_at(early_places), span)
    first = regroup([early[0], across(early[1], "xfer", 1, "early")])
    middle_out = pack_all(values, scales, request_at(middle_places), span, first[0])
    second = regroup(
        [across(held(early[k], first[0]), "xfer", k, "early") for k in range(2, groups)]
    )

    ids = jnp.arange(requests, dtype=jnp.int32)
    source = ids // per_group
    mine = decode_of == me
    before = ids[None, :] < ids[:, None]
    rank = jnp.sum(
        (
            before
            & (decode_of[None, :] == decode_of[:, None])
            & (source[None, :] == source[:, None])
        ).astype(jnp.int32),
        axis=1,
    )
    slot = jnp.sum((before & mine[None, :]).astype(jnp.int32), axis=1)
    is_late, is_last = rank >= sure, rank >= pair_share
    in_middle = mine & is_late & ~is_last
    late_rank = jnp.where(is_last, jnp.sum(in_middle.astype(jnp.int32)), 0) + jnp.sum(
        (before & ((mine & is_late)[None, :] & (is_last[None, :] == is_last[:, None]))).astype(
            jnp.int32
        ),
        axis=1,
    )
    offset = source ^ me
    first_place = offset * half_sure + rank % half_sure
    late_chunk, late_rest = late_rank // (2 * late_half), late_rank % (2 * late_half)
    late_place = late_start + late_chunk * late_half + late_rest % late_half
    side = jnp.where(is_late, late_rest // late_half, rank // half_sure) ^ parity
    place = side * half + jnp.where(is_late, late_place, first_place)
    hit = mine[None, :] & (place[None, :] == here[:, None])

    def at_place(values):
        return jnp.sum(jnp.where(hit, values[None, :], 0), axis=1)

    replicas = lax.axis_size("groups") * groups
    replica = lax.axis_index("groups") * groups + me
    slots = at_place(slot)
    lengths = at_place(kv_lengths)
    late_which = at_place(is_last.astype(jnp.int32)).reshape(2, half)[:, late_start:]
    late_index = at_place(source * late + (rank - sure) % late).reshape(2, half)[:, late_start:]
    place_of_slot = jnp.sum(
        jnp.where(mine[None, :] & (slot[None, :] == here[:, None]), place[None, :], 0), axis=1
    )

    def send_keys(own_keys, far_keys, name, *waits):
        own_keys, far_keys = held(own_keys, *waits), held(far_keys, *waits)
        return [own_keys] + [
            across(far_keys if k % 2 else own_keys, "tensor", k, name) for k in range(1, shards)
        ]

    def land(out):
        arrived = lax.all_to_all(out, "xfer", 0, 0, tiled=True)
        return arrived.reshape(groups * late, row_width, span)

    replicas = lax.axis_size("groups") * groups
    replica = lax.axis_index("groups") * groups + me

    def piece_of(weights, *waits):
        flat = weights.reshape(-1, weights.shape[-1])
        piece = cut(flat, replicas, replica, *waits)
        return across(piece, "tensor", 1, "piece")

    def between_chips(piece):
        sent = {0: piece}
        for t in range(2, replicas, 2):
            sent[t] = across(piece, ("groups", "xfer"), t, "chips")
        return sent

    def between_cores(sent):
        for t in range(0, replicas, 2):
            sent[t + 1] = across(sent[t], "xfer", 1, "cores")
        return sent

    def joined(sent, weights):
        pieces = [sent[t] for t in range(replicas)]
        return in_order(pieces, replica).reshape(weights.shape)

    def take(x, index):
        return jnp.take(x, index, axis=0, mode="clip")

    def attend_chunk(chunk, keys, waits):
        start = starts[chunk]
        live = lengths[start : start + sizes[chunk]]
        scalars = jnp.concatenate([shard[None], live]).astype(jnp.int32)
        queries = [latent_own, latent_far, rope_own, rope_far]
        return attend(scalars, start, queries, keys, new_own, steps, score_scale, waits)

    def project(latent, weights):
        size = latent.shape[0]
        out = jnp.einsum(
            "rthc,hcv->rthv",
            latent.reshape(size, steps, heads_here, latent_width),
            weights,
            preferred_element_type=jnp.float32,
        )
        return out.astype(jnp.bfloat16).reshape(size, steps, heads_here * value_width)

    def absorb(nope, weights):
        heads = nope.reshape(half, steps, heads_here, nope_width)
        latent = jnp.einsum("rthn,hnc->rthc", heads, weights, preferred_element_type=jnp.float32)
        return latent.astype(jnp.bfloat16).reshape(half, steps * heads_here, latent_width)

    def rotary(rope):
        return rope.reshape(half, steps * heads_here, rope_width)

    keys = [send_keys(*first, "keys0")]
    wk_piece = piece_of(wk_up, first[0])
    middle_in = land(held(middle_out, second[0]))
    keys.append(send_keys(*second, "keys1", *keys[0][1:], wk_piece))
    wk_sent = between_chips(held(wk_piece, *keys[0][1:]))
    wv_piece = piece_of(wv_up, *keys[0][1:])
    last_out = pack_all(values, scales, request_at(last_places), span, *keys[0][1:])
    third = select_blocks(
        [middle_in], jnp.zeros_like(late_which[:, :late_half]), late_index[:, :late_half]
    )
    keys.append(send_keys(*third, "keys2", *keys[1][1:], *list(wk_sent.values())[1:], wv_piece))
    wk_sent[0] = held(wk_sent[0], *keys[1][1:])
    for t in range(2, replicas, 2):
        wk_sent[t] = held(wk_sent[t], *keys[1][1:])
    wk_sent = between_cores(wk_sent)
    wv_sent = between_chips(held(wv_piece, *keys[1][1:]))
    last_in = land(held(last_out, *keys[1][1:]))
    nope_own, nope_far, rope_own, rope_far = by_side(
        [q_nope, q_rope], slots.reshape(2, half), *keys[1][1:]
    )
    nope_far = across(nope_far, "tensor", 1, "nope")
    rope_far = across(rope_far, "tensor", 1, "rope")
    new_own = take(new_kv, slots[:half])
    new_own = jnp.pad(new_own, ((0, 0), (0, NEW_ROWS - steps), (0, 0)))
    fourth = select_blocks(
        [middle_in, last_in], late_which[:, late_half:], late_index[:, late_half:]
    )
    before_fourth = keys[2][1:] + [wk_sent[t] for t in range(1, replicas, 2)]
    before_fourth += [wv_sent[t] for t in range(2, replicas, 2)] + [nope_far, rope_far]
    keys.append(send_keys(*fourth, "keys3", *before_fourth))
    for t in range(0, replicas, 2):
        wv_sent[t] = held(wv_sent[t], *keys[2][1:])
    wv_sent = between_cores(wv_sent)
    wk_far, wv_far = joined(wk_sent, wk_up), joined(wv_sent, wv_up)
    latent_own, latent_far = absorb(nope_own, wk_up), absorb(nope_far, wk_far)
    rope_own, rope_far = rotary(rope_own), rotary(rope_far)
    latents = []
    for chunk in range(4):
        latents.append(attend_chunk(chunk, keys[chunk], [x for x, _ in latents[-1:]]))
    far_heads = [across(project(far, wv_far), "tensor", 1, "heads") for _, far in latents]
    own_heads = [project(own, wv_up) for own, _ in latents]
    head_out = take(jnp.concatenate(own_heads + far_heads, axis=0), place_of_slot)
    partial = jnp.dot(
        head_out.reshape(per_group * steps, -1), w_out, preferred_element_type=jnp.float32
    ).astype(jnp.bfloat16)
    parts = lax.all_to_all(
        partial.reshape(shards, out_rows, steps, -1), "tensor", 0, 0, tiled=True
    )
    return jnp.sum(parts.astype(jnp.float32), axis=0).astype(jnp.bfloat16)


def solution(mesh):
    return jax.shard_map(
        local,
        mesh=mesh,
        in_specs=(
            P(("groups", "xfer", "tensor"), None),
            P(("groups", "xfer", "tensor"), None),
            P("groups"),
            P("groups"),
            P(("groups", "xfer"), None, "tensor"),
            P(("groups", "xfer"), None, "tensor"),
            P(("groups", "xfer"), None, None),
            P("tensor", None, None),
            P("tensor", None, None),
            P("tensor", None),
        ),
        out_specs=P(("groups", "xfer", "tensor"), None, None),
        check_vma=False,
    )
```

```python
import math

import jax
import jax.numpy as jnp
from jax import lax
from jax.experimental import pallas as pl
from jax.experimental.pallas import tpu as pltpu
from jax.sharding import PartitionSpec as P

MASKED_SCORE = -1e30
NEW_ROWS = 16


SHORT = pl.CostEstimate(flops=1024, bytes_accessed=1024, transcendentals=0)


def pack_kernel(groups, blocks, index_ref, *refs):
    values, scales = refs[:groups], refs[groups : 2 * groups]
    outs = refs[len(refs) - groups :]
    for value_ref, scale_ref, out_ref in zip(values, scales, outs):
        width = value_ref.shape[-2]
        latent_width = blocks * 128
        span = value_ref.shape[-1]
        factor = scale_ref[...].reshape(blocks, span).astype(jnp.float32)
        for block in range(blocks):
            rows = slice(block * 128, (block + 1) * 128)
            part = value_ref[..., rows, :].reshape(128, span).astype(jnp.float32)
            out_ref[0, rows, :] = (part * factor[block : block + 1, :]).astype(jnp.bfloat16)
        rest = value_ref[..., latent_width:width, :]
        out_ref[0, latent_width:width, :] = rest.reshape(width - latent_width, span)


def pack(values, scales, index, span, waits=()):
    groups, count = index.shape
    width, blocks = values.shape[-2], scales.shape[-2]

    def spec(rows, group):
        if values.ndim == 2:
            return pl.BlockSpec((rows, span), lambda n, index_ref: (0, index_ref[group, n]))
        return pl.BlockSpec((1, rows, span), lambda n, index_ref: (index_ref[group, n], 0, 0))

    return pl.pallas_call(
        lambda *refs: pack_kernel(groups, blocks, *refs),
        grid_spec=pltpu.PrefetchScalarGridSpec(
            num_scalar_prefetch=1,
            grid=(count,),
            in_specs=[spec(width, g) for g in range(groups)]
            + [spec(blocks, g) for g in range(groups)]
            + [pl.BlockSpec(memory_space=pl.ANY)] * len(waits),
            out_specs=[pl.BlockSpec((1, width, span), lambda n, index_ref: (n, 0, 0))] * groups,
        ),
        out_shape=[jax.ShapeDtypeStruct((count, width, span), jnp.bfloat16)] * groups,
        cost_estimate=SHORT,
    )(index, *([values] * groups), *([scales] * groups), *waits)


def pack_all(values, scales, index, span, *waits):
    groups, count = index.shape
    width, blocks = values.shape[-2], scales.shape[-2]

    def kernel(index_ref, *refs):
        outs = [refs[-1].at[g] for g in range(groups)]
        pack_kernel(groups, blocks, index_ref, *refs[: 2 * groups], *outs)

    def spec(rows, group):
        if values.ndim == 2:
            return pl.BlockSpec((rows, span), lambda n, index_ref: (0, index_ref[group, n]))
        return pl.BlockSpec((1, rows, span), lambda n, index_ref: (index_ref[group, n], 0, 0))

    return pl.pallas_call(
        kernel,
        grid_spec=pltpu.PrefetchScalarGridSpec(
            num_scalar_prefetch=1,
            grid=(count,),
            in_specs=[spec(width, g) for g in range(groups)]
            + [spec(blocks, g) for g in range(groups)]
            + [pl.BlockSpec(memory_space=pl.ANY)] * len(waits),
            out_specs=pl.BlockSpec(
                (groups, 1, width, span), lambda n, index_ref: (0, n, 0, 0)
            ),
        ),
        out_shape=jax.ShapeDtypeStruct((groups, count, width, span), jnp.bfloat16),
        cost_estimate=SHORT,
    )(index, *([values] * groups), *([scales] * groups), *waits)


def held(arrays, *waits):
    def kernel(*refs):
        pass

    anywhere = pl.BlockSpec(memory_space=pl.ANY)
    return pl.pallas_call(
        kernel,
        in_specs=[anywhere] * (len(arrays) + len(waits)),
        out_specs=[anywhere] * len(arrays),
        out_shape=[jax.ShapeDtypeStruct(x.shape, x.dtype) for x in arrays],
        input_output_aliases={i: i for i in range(len(arrays))},
        cost_estimate=SHORT,
    )(*arrays, *waits)


def regroup_kernel(count, *refs):
    refs = refs[: 2 * count] + refs[-2:]
    for k in range(count):
        refs[2 * count][k, 0] = refs[k][0]
        refs[2 * count + 1][k, 0] = refs[count + k][0]


def regroup(landed, *waits):
    count, (rows, width, span) = len(landed), landed[0].shape
    half = rows // 2
    own = pl.BlockSpec((1, width, span), lambda n: (n, 0, 0))
    far = pl.BlockSpec((1, width, span), lambda n: (half + n, 0, 0))
    outs = pl.pallas_call(
        lambda *refs: regroup_kernel(count, *refs),
        grid=(half,),
        in_specs=[own] * count
        + [far] * count
        + [pl.BlockSpec(memory_space=pl.ANY)] * len(waits),
        out_specs=[pl.BlockSpec((count, 1, width, span), lambda n: (0, n, 0, 0))] * 2,
        out_shape=[jax.ShapeDtypeStruct((count, half, width, span), jnp.bfloat16)] * 2,
        cost_estimate=SHORT,
    )(*landed, *landed, *waits)
    return tuple(x.reshape(count * half, width, span) for x in outs)


def regroup_arrived(arrived, offsets, me):
    rows, width, span = arrived.shape[1:]
    half, count = rows // 2, len(offsets)

    def spec(offset, first):
        return pl.BlockSpec(
            (1, 1, width, span), lambda n, me_ref: (me_ref[0] ^ offset, first + n, 0, 0)
        )

    def kernel(me_ref, *refs):
        for side in range(2):
            for k in range(count):
                refs[2 * count + side][k, 0] = refs[side * count + k][0, 0]

    outs = pl.pallas_call(
        kernel,
        grid_spec=pltpu.PrefetchScalarGridSpec(
            num_scalar_prefetch=1,
            grid=(half,),
            in_specs=[spec(k, 0) for k in offsets] + [spec(k, half) for k in offsets],
            out_specs=[pl.BlockSpec((count, 1, width, span), lambda n, me_ref: (0, n, 0, 0))] * 2,
        ),
        out_shape=[jax.ShapeDtypeStruct((count, half, width, span), jnp.bfloat16)] * 2,
        cost_estimate=SHORT,
    )(me[None], *([arrived] * (2 * count)))
    return tuple(x.reshape(count * half, width, span) for x in outs)


def select_kernel(sources, which_ref, index_ref, *refs):
    n = pl.program_id(0)
    refs = refs[: 2 * sources] + refs[-2:]
    for side in range(2):
        for source in range(sources):

            @pl.when(which_ref[side, n] == source)
            def _(side=side, source=source):
                refs[2 * sources + side][...] = refs[side * sources + source][...]


def select_blocks(arrived, which, index, *waits):
    count = index.shape[1]
    width, span = arrived[0].shape[1:]

    def pick(side, source):
        def place(n, which_ref, index_ref):
            return jnp.where(which_ref[side, n] == source, index_ref[side, n], 0), 0, 0

        return pl.BlockSpec((1, width, span), place)

    return pl.pallas_call(
        lambda *refs: select_kernel(len(arrived), *refs),
        grid_spec=pltpu.PrefetchScalarGridSpec(
            num_scalar_prefetch=2,
            grid=(count,),
            in_specs=[pick(i, j) for i in range(2) for j in range(len(arrived))]
            + [pl.BlockSpec(memory_space=pl.ANY)] * len(waits),
            out_specs=[pl.BlockSpec((1, width, span), lambda n, *refs: (n, 0, 0))] * 2,
        ),
        out_shape=[jax.ShapeDtypeStruct((count, width, span), jnp.bfloat16)] * 2,
        cost_estimate=SHORT,
    )(which, index, *arrived, *arrived, *waits)


def cut(wk, wv, pieces, which, *waits):
    width, narrow = wk.shape[1], wv.shape[1]
    rows, folds = wk.shape[0] // pieces, width // narrow

    def kernel(which_ref, wk_ref, wv_ref, *refs):
        refs[-1][:rows, :] = wk_ref[...]
        for fold in range(folds):
            columns = slice(fold * narrow, (fold + 1) * narrow)
            refs[-1][rows:, columns] = wv_ref[fold * rows : (fold + 1) * rows, :]

    def block(rows, columns):
        return pl.BlockSpec((rows, columns), lambda n, which_ref: (which_ref[0], 0))

    return pl.pallas_call(
        kernel,
        grid_spec=pltpu.PrefetchScalarGridSpec(
            num_scalar_prefetch=1,
            grid=(1,),
            in_specs=[block(rows, width), block(folds * rows, narrow)]
            + [pl.BlockSpec(memory_space=pl.ANY)] * len(waits),
            out_specs=pl.BlockSpec((2 * rows, width), lambda n, which_ref: (0, 0)),
        ),
        out_shape=jax.ShapeDtypeStruct((2 * rows, width), wk.dtype),
        cost_estimate=SHORT,
    )(which[None], wk, wv, *waits)


def doubled(near, far):
    count, rows, width = near.shape

    def kernel(near_ref, far_ref, out_ref):
        out_ref[0] = near_ref[...]
        out_ref[1] = far_ref[...]

    spec = pl.BlockSpec((1, rows, width), lambda n: (n, 0, 0))
    out = pl.pallas_call(
        kernel,
        grid=(count,),
        in_specs=[spec] * 2,
        out_specs=pl.BlockSpec((2, 1, rows, width), lambda n: (0, n, 0, 0)),
        out_shape=jax.ShapeDtypeStruct((2, count, rows, width), near.dtype),
        cost_estimate=SHORT,
    )(near, far)
    return out.reshape(2 * count, rows, width)


def in_order(near, far, replica, narrow, *waits):
    count, rows, width = near.shape
    rows, folds = rows // 2, width // narrow

    def pick(n, replica_ref):
        return (n ^ replica_ref[0]) // 2, 0, 0

    def kernel(replica_ref, near_ref, far_ref, *refs):
        wk_out, wv_out = refs[-2:]
        odd = (pl.program_id(0) ^ replica_ref[0]) & 1

        def put(source):
            wk_out[0] = source[0, :rows, :]
            for fold in range(folds):
                columns = slice(fold * narrow, (fold + 1) * narrow)
                wv_out[0, fold * rows : (fold + 1) * rows, :] = source[0, rows:, columns]

        @pl.when(odd == 0)
        def _():
            put(near_ref)

        @pl.when(odd == 1)
        def _():
            put(far_ref)

    return pl.pallas_call(
        kernel,
        grid_spec=pltpu.PrefetchScalarGridSpec(
            num_scalar_prefetch=1,
            grid=(2 * count,),
            in_specs=[pl.BlockSpec((1, 2 * rows, width), pick)] * 2
            + [pl.BlockSpec(memory_space=pl.ANY)] * len(waits),
            out_specs=[
                pl.BlockSpec((1, rows, width), lambda n, replica_ref: (n, 0, 0)),
                pl.BlockSpec((1, folds * rows, narrow), lambda n, replica_ref: (n, 0, 0)),
            ],
        ),
        out_shape=[
            jax.ShapeDtypeStruct((2 * count, rows, width), near.dtype),
            jax.ShapeDtypeStruct((2 * count, folds * rows, narrow), near.dtype),
        ],
        cost_estimate=SHORT,
    )(replica[None], near, far, *waits)


def by_side(arrays, index, *waits):
    count = index.shape[1]
    steps = arrays[0].shape[1]
    width = sum(x.shape[2] for x in arrays)

    def kernel(index_ref, *refs):
        outs, staged = refs[-3:-1], refs[-1]
        for side in range(2):
            first = 0
            for x_ref in refs[: len(arrays)]:
                columns = slice(first, first + x_ref.shape[2])
                first += x_ref.shape[2]
                for n in range(count):
                    rows = x_ref[index_ref[side, n]].astype(jnp.float32)
                    staged[n * steps : (n + 1) * steps, columns] = rows
            outs[side][...] = staged[...].astype(outs[side].dtype)

    vmem = pl.BlockSpec(memory_space=pltpu.VMEM)
    return pl.pallas_call(
        kernel,
        in_specs=[pl.BlockSpec(memory_space=pltpu.SMEM)]
        + [vmem] * len(arrays)
        + [pl.BlockSpec(memory_space=pl.ANY)] * len(waits),
        out_specs=[vmem] * 2,
        out_shape=[jax.ShapeDtypeStruct((count * steps, width), arrays[0].dtype)] * 2,
        scratch_shapes=[pltpu.VMEM((count * steps, width), jnp.float32)],
        compiler_params=pltpu.CompilerParams(vmem_limit_bytes=24 * 1024 * 1024),
        cost_estimate=SHORT,
    )(index, *arrays, *waits)


def absorb(queries, weights, steps, *waits):
    rows = queries.shape[0]
    heads, nope_width, latent_width = weights.shape
    rope_width = queries.shape[1] // heads - nope_width

    def kernel(queries_ref, weights_ref, *refs):
        latent_out, rope_out, latent_rows, rope_rows = refs[len(waits) :]
        for head in range(heads):
            place = pl.ds(head, rows, stride=heads)
            columns = slice(head * nope_width, (head + 1) * nope_width)
            product = jnp.dot(
                queries_ref[:, columns], weights_ref[head], preferred_element_type=jnp.float32
            )
            for block in range(latent_width // 128):
                latent_rows[block, place, :] = product[:, block * 128 : (block + 1) * 128]
            first = heads * nope_width + head * rope_width
            part = queries_ref[:, first : first + rope_width].astype(jnp.float32)
            rope_rows[place, :] = jnp.concatenate([part] * (128 // rope_width), axis=1)
        for block in range(latent_width // 128):
            columns = slice(block * 128, (block + 1) * 128)
            latent_out[:, columns] = latent_rows[block].astype(jnp.bfloat16)
        rope_out[...] = rope_rows[:, :rope_width].astype(jnp.bfloat16)

    vmem = pl.BlockSpec(memory_space=pltpu.VMEM)
    latent, rotary = pl.pallas_call(
        kernel,
        in_specs=[vmem] * 2 + [pl.BlockSpec(memory_space=pl.ANY)] * len(waits),
        out_specs=[vmem] * 2,
        out_shape=[
            jax.ShapeDtypeStruct((rows * heads, latent_width), jnp.bfloat16),
            jax.ShapeDtypeStruct((rows * heads, rope_width), jnp.bfloat16),
        ],
        scratch_shapes=[
            pltpu.VMEM((latent_width // 128, rows * heads, 128), jnp.float32),
            pltpu.VMEM((rows * heads, 128), jnp.float32),
        ],
        compiler_params=pltpu.CompilerParams(vmem_limit_bytes=24 * 1024 * 1024),
        cost_estimate=SHORT,
    )(queries, weights, *waits)
    slots = rows // steps
    return (
        latent.reshape(slots, steps * heads, latent_width),
        rotary.reshape(slots, steps * heads, rope_width),
    )


def attend_kernel(shards, steps, score_scale, scalars, *refs):
    queries = refs[:4]
    keys = refs[4 : 4 + shards]
    new_ref, own_out, other_out = refs[4 + shards], refs[-2], refs[-1]
    own_latent, other_latent, own_rope, other_rope = queries
    latent_width = own_latent.shape[2]
    span = keys[0].shape[2]
    length = scalars[1 + pl.program_id(0)]
    shard = scalars[0]
    key_columns = jnp.concatenate([ref[0] for ref in keys], axis=1)
    new_rows = new_ref[0]
    query = jnp.concatenate([own_latent[0], other_latent[0]], axis=0)
    rope = jnp.concatenate([own_rope[0], other_rope[0]], axis=0)
    across = (((1,), (1,)), ((), ()))
    along = (((1,), (0,)), ((), ()))

    def product(left, right, contract):
        return lax.dot_general(left, right, contract, preferred_element_type=jnp.float32)

    cache_scores = score_scale * (
        product(query, key_columns[:latent_width], along)
        + product(rope, key_columns[latent_width:], along)
    )
    new_scores = score_scale * (
        product(query, new_rows[:, :latent_width], across)
        + product(rope, new_rows[:, latent_width:], across)
    )
    column = lax.broadcasted_iota(jnp.int32, cache_scores.shape, 1)
    position = (shard ^ (column // span)) * span + column % span
    cache_live = position < length
    half = own_latent.shape[1]
    row = lax.broadcasted_iota(jnp.int32, new_scores.shape, 0)
    step = (row % half) // (half // steps)
    new_live = lax.broadcasted_iota(jnp.int32, new_scores.shape, 1) <= step
    cache_scores = jnp.where(cache_live, cache_scores, MASKED_SCORE)
    new_scores = jnp.where(new_live, new_scores, MASKED_SCORE)
    top = jnp.maximum(
        jnp.max(cache_scores, axis=1, keepdims=True), jnp.max(new_scores, axis=1, keepdims=True)
    )
    cache_weights = jnp.where(cache_live, jnp.exp(cache_scores - top), 0.0)
    new_weights = jnp.where(new_live, jnp.exp(new_scores - top), 0.0)
    weight_sum = jnp.sum(cache_weights, axis=1, keepdims=True) + jnp.sum(
        new_weights, axis=1, keepdims=True
    )
    mixed = product(
        cache_weights.astype(jnp.bfloat16), key_columns[:latent_width], across
    ) + product(new_weights.astype(jnp.bfloat16), new_rows[:, :latent_width], along)
    latent = (mixed / weight_sum).astype(jnp.bfloat16)
    own_out[0] = latent[:half]
    other_out[0] = latent[half:]


def attend(scalars, start, queries, keys, new_rows, steps, score_scale, waits):
    count, (half, latent_width) = keys[0].shape[0], queries[0].shape[1:]
    rope_width = queries[2].shape[2]
    width, span = keys[0].shape[1:]
    shards = len(keys)

    def block(rows, columns, first=0):
        return pl.BlockSpec((1, rows, columns), lambda n, scalars: (first + n, 0, 0))

    return pl.pallas_call(
        lambda *refs: attend_kernel(shards, steps, score_scale, *refs),
        grid_spec=pltpu.PrefetchScalarGridSpec(
            num_scalar_prefetch=1,
            grid=(count,),
            in_specs=[block(half, latent_width, start)] * 2
            + [block(half, rope_width, start)] * 2
            + [block(width, span)] * shards
            + [block(NEW_ROWS, width, start)]
            + [pl.BlockSpec(memory_space=pl.ANY)] * len(waits),
            out_specs=[block(half, latent_width)] * 2,
        ),
        out_shape=[jax.ShapeDtypeStruct((count, half, latent_width), jnp.bfloat16)] * 2,
        compiler_params=pltpu.CompilerParams(vmem_limit_bytes=32 * 1024 * 1024),
        cost_estimate=SHORT,
    )(scalars, *queries, *keys, new_rows, *waits)


def output(head_out, row_of, w_out, shards):
    rows, columns = row_of.shape[0], w_out.shape[1]
    depth, width = w_out.shape[0], 512
    while columns % width:
        width //= 2

    def kernel(row_ref, *refs):
        heads, w_ref = refs[: len(head_out)], refs[len(head_out)]
        outs, ordered = refs[len(head_out) + 1 : -1], refs[-1]

        @pl.when(pl.program_id(0) == 0)
        def _():
            place = lax.broadcasted_iota(jnp.int32, (rows, rows), 1)
            chosen = (place == row_ref[...]).astype(jnp.bfloat16)
            stacked = jnp.concatenate([ref[...] for ref in heads], axis=0)
            ordered[...] = jnp.dot(
                chosen, stacked, preferred_element_type=jnp.float32
            ).astype(jnp.bfloat16)

        result = jnp.dot(ordered[...], w_ref[...], preferred_element_type=jnp.float32)
        share = rows // shards
        for k in range(shards):
            outs[k][...] = result[k * share : (k + 1) * share].astype(jnp.bfloat16)

    def whole(x):
        return pl.BlockSpec(x.shape, lambda n: (0, 0))

    return pl.pallas_call(
        kernel,
        grid=(columns // width,),
        in_specs=[whole(row_of)]
        + [whole(x) for x in head_out]
        + [pl.BlockSpec((depth, width), lambda n: (0, n))],
        out_specs=[pl.BlockSpec((rows // shards, width), lambda n: (0, n))] * shards,
        out_shape=[jax.ShapeDtypeStruct((rows // shards, columns), jnp.bfloat16)] * shards,
        scratch_shapes=[pltpu.VMEM((rows, depth), jnp.bfloat16)],
        compiler_params=pltpu.CompilerParams(vmem_limit_bytes=30 * 1024 * 1024),
        cost_estimate=pl.CostEstimate(
            flops=2 * rows * depth * columns,
            bytes_accessed=2 * depth * columns,
            transcendentals=0,
        ),
    )(row_of, *head_out, w_out)


def local(kv_values, kv_scales, decode_of, kv_lengths, q_nope, q_rope, new_kv, wk_up, wv_up, w_out):
    groups = lax.axis_size("xfer")
    shards = lax.axis_size("tensor")
    me = lax.axis_index("xfer")
    shard = lax.axis_index("tensor")
    parity = shard % 2
    requests = decode_of.shape[0]
    per_group = requests // groups
    row_width = kv_values.shape[1]
    span = kv_values.shape[0] // per_group
    pair_share = per_group // groups
    pair_room = pair_share + pair_share // 2
    sure = pair_share - pair_share // 2
    late = pair_share // 2
    heads_here, nope_width, latent_width = wk_up.shape
    value_width = wv_up.shape[2]
    steps = q_nope.shape[1]
    rope_width = q_rope.shape[2] // heads_here
    score_scale = 1.0 / math.sqrt(nope_width + rope_width)
    out_rows = per_group // shards
    half = per_group // 2
    half_sure = sure // 2
    late_half = (per_group - groups * sure) // 4
    sizes = [2 * half_sure, (groups - 2) * half_sure, late_half, late_half]
    starts = [0, sizes[0], sizes[0] + sizes[1], sizes[0] + sizes[1] + sizes[2]]
    late_start = starts[2]

    def across(x, axis, offset, name="other"):
        with jax.named_scope(f"{name}_{axis if isinstance(axis, str) else 'both'}{offset}"):
            return lax.ppermute(x, axis, [(i, i ^ offset) for i in range(lax.axis_size(axis))])

    dest_here = lax.dynamic_slice_in_dim(decode_of, me * per_group, per_group)
    here = jnp.arange(per_group, dtype=jnp.int32)
    rank_here = jnp.sum(
        ((dest_here[:, None] == dest_here[None, :]) & (here[None, :] < here[:, None])).astype(
            jnp.int32
        ),
        axis=1,
    )
    place_here = dest_here * pair_room + rank_here
    early_ranks = jnp.arange(sure, dtype=jnp.int32)
    early_ranks = (early_ranks + parity * half_sure) % sure
    offsets = jnp.arange(groups, dtype=jnp.int32)
    early_places = (me ^ offsets)[:, None] * pair_room + early_ranks[None, :]
    late_ranks = jnp.arange(late, dtype=jnp.int32)
    middle_places = offsets[:, None] * pair_room + sure + late_ranks[None, :]
    last_places = middle_places + late

    def request_at(places):
        hit = places[..., None] == place_here
        return jnp.sum(jnp.where(hit, here, 0), axis=-1)

    if span % 128 == 0:
        values, scales = kv_values.T, kv_scales.T
    else:
        values = kv_values.reshape(per_group, span, -1).swapaxes(1, 2)
        scales = kv_scales.reshape(per_group, span, -1).swapaxes(1, 2)
    near = pack(values, scales, request_at(early_places[:2]), span)
    first = regroup([near[0], across(near[1], "xfer", 1, "early")])
    far_places = offsets[:, None] * pair_room + early_ranks[None, :]
    early_out = pack_all(values, scales, request_at(far_places), span, first[0])

    ids = jnp.arange(requests, dtype=jnp.int32)
    source = ids // per_group
    mine = decode_of == me
    before = ids[None, :] < ids[:, None]
    rank = jnp.sum(
        (
            before
            & (decode_of[None, :] == decode_of[:, None])
            & (source[None, :] == source[:, None])
        ).astype(jnp.int32),
        axis=1,
    )
    slot = jnp.sum((before & mine[None, :]).astype(jnp.int32), axis=1)
    is_late, is_last = rank >= sure, rank >= pair_share
    in_middle = mine & is_late & ~is_last
    late_rank = jnp.where(is_last, jnp.sum(in_middle.astype(jnp.int32)), 0) + jnp.sum(
        (before & ((mine & is_late)[None, :] & (is_last[None, :] == is_last[:, None]))).astype(
            jnp.int32
        ),
        axis=1,
    )
    offset = source ^ me
    first_place = offset * half_sure + rank % half_sure
    late_chunk, late_rest = late_rank // (2 * late_half), late_rank % (2 * late_half)
    late_place = late_start + late_chunk * late_half + late_rest % late_half
    side = jnp.where(is_late, late_rest // late_half, rank // half_sure) ^ parity
    place = side * half + jnp.where(is_late, late_place, first_place)
    hit = mine[None, :] & (place[None, :] == here[:, None])

    def at_place(values):
        return jnp.sum(jnp.where(hit, values[None, :], 0), axis=1)

    replicas = lax.axis_size("groups") * groups
    replica = lax.axis_index("groups") * groups + me
    slots = at_place(slot)
    lengths = at_place(kv_lengths)
    late_which = at_place(is_last.astype(jnp.int32)).reshape(2, half)[:, late_start:]
    late_index = at_place(source * late + (rank - sure) % late).reshape(2, half)[:, late_start:]
    place_of_slot = jnp.sum(
        jnp.where(mine[None, :] & (slot[None, :] == here[:, None]), place[None, :], 0), axis=1
    )

    def send_keys(chunk, name, waits=(), carried=()):
        if waits:
            own_keys, far_keys, *carried = held([*chunk, *carried], *waits)
        else:
            own_keys, far_keys = chunk
        keys = [own_keys] + [
            across(far_keys if k % 2 else own_keys, "tensor", k, name) for k in range(1, shards)
        ]
        return keys, *carried

    def land(out):
        return lax.all_to_all(out, "xfer", 0, 0, tiled=True)

    def flat(arrived):
        return arrived.reshape(groups * late, row_width, span)

    replicas = lax.axis_size("groups") * groups
    replica = lax.axis_index("groups") * groups + me

    def take(x, index):
        return jnp.take(x, index, axis=0, mode="clip")

    def attend_chunk(chunk, keys, waits):
        start = starts[chunk]
        live = lengths[start : start + sizes[chunk]]
        scalars = jnp.concatenate([shard[None], live]).astype(jnp.int32)
        queries = [latent_own, latent_far, rope_own, rope_far]
        return attend(scalars, start, queries, keys, new_own, steps, score_scale, waits)

    def project(latent, weights):
        size = latent.shape[0]
        out = jnp.einsum(
            "rthc,hcv->rthv",
            latent.reshape(size, steps, heads_here, latent_width),
            weights,
            preferred_element_type=jnp.float32,
        )
        return out.astype(jnp.bfloat16).reshape(size, steps, heads_here * value_width)

    wk, wv = (x.reshape(-1, x.shape[-1]) for x in (wk_up, wv_up))
    hops = [("xfer", 1 << i) for i in range(1, groups.bit_length() - 1)]
    hops += [("groups", 1 << i) for i in range((replicas // groups).bit_length() - 1)]
    keys = list(send_keys(first, "keys0"))
    stack = across(cut(wk, wv, replicas, replica, first[0]), "tensor", 1, "weights")[None]
    second = regroup_arrived(land(early_out), range(2, groups), me)
    sent, stack = send_keys(second, "keys1", keys[0][1:], [stack])
    keys.append(sent)
    queries_own, queries_far = by_side([q_nope, q_rope], slots.reshape(2, half), *keys[0][1:])
    queries_far = across(queries_far, "tensor", 1, "queries")
    middle_out = pack_all(values, scales, request_at(middle_places), span, second[0])
    middle_in = flat(land(middle_out))
    last_out = pack_all(values, scales, request_at(last_places), span, *keys[0][1:])
    for axis, offset in hops[:-1]:
        stack = doubled(stack, across(stack, axis, offset, "weights"))
    third = select_blocks(
        [middle_in], jnp.zeros_like(late_which[:, :late_half]), late_index[:, :late_half]
    )
    latent_own, rope_own = absorb(queries_own, wk_up, steps, third[0])
    sent, stack = send_keys(third, "keys2", [*keys[1][1:], queries_far, latent_own, last_out], [stack])
    keys.append(sent)
    last_in = flat(land(last_out))
    for axis, offset in hops[-1:]:
        stack = doubled(stack, across(stack, axis, offset, "weights"))
    fourth = select_blocks(
        [middle_in, last_in], late_which[:, late_half:], late_index[:, late_half:]
    )
    sent, stack = send_keys(fourth, "keys3", keys[2][1:], [stack])
    keys.append(sent)
    wk_far, wv_far = in_order(stack, across(stack, "xfer", 1, "weights"), replica, wv.shape[-1])
    wk_far, wv_far = wk_far.reshape(wk_up.shape), wv_far.reshape(wv_up.shape)
    latent_far, rope_far = absorb(queries_far, wk_far, steps)
    new_own = take(new_kv, slots[:half])
    new_own = jnp.pad(new_own, ((0, 0), (0, NEW_ROWS - steps), (0, 0)))
    latents, own_heads, far_heads = [], [], []
    for chunk in range(4):
        waits = [x for x, _ in latents[-1:]] if chunk < 3 else own_heads + far_heads
        own, far = attend_chunk(chunk, keys[chunk], waits)
        latents.append((own, far))
        far_heads.append(project(far, wv_far))
        own_heads.append(project(own, wv_up))
    far_heads = [across(x, "tensor", 1, "heads") for x in far_heads]
    head_out = [x.reshape(-1, x.shape[-1]) for x in own_heads + far_heads]
    row = jnp.arange(per_group * steps, dtype=jnp.int32)
    slot_of_row = ((shard ^ (row // (out_rows * steps))) * out_rows * steps) + row % (
        out_rows * steps
    )
    row_of = jnp.take(place_of_slot, slot_of_row // steps, mode="clip") * steps + row % steps
    parts = output(head_out, row_of[:, None], w_out, shards)
    parts = [parts[0]] + [across(parts[k], "tensor", k, "output") for k in range(1, shards)]
    summed = sum(x.astype(jnp.float32) for x in parts).astype(jnp.bfloat16)
    return summed.reshape(out_rows, steps, -1)


def solution(mesh):
    return jax.shard_map(
        local,
        mesh=mesh,
        in_specs=(
            P(("groups", "xfer", "tensor"), None),
            P(("groups", "xfer", "tensor"), None),
            P("groups"),
            P("groups"),
            P(("groups", "xfer"), None, "tensor"),
            P(("groups", "xfer"), None, "tensor"),
            P(("groups", "xfer"), None, None),
            P("tensor", None, None),
            P("tensor", None, None),
            P("tensor", None),
        ),
        out_specs=P(("groups", "xfer", "tensor"), None, None),
        check_vma=False,
    )
```

```python
import math

import jax
import jax.numpy as jnp
from jax import lax
from jax.experimental import pallas as pl
from jax.experimental.pallas import tpu as pltpu
from jax.sharding import PartitionSpec as P

MASKED_SCORE = -1e30
NEW_ROWS = 16


SHORT = pl.CostEstimate(flops=1024, bytes_accessed=1024, transcendentals=0)


def pack_kernel(groups, blocks, index_ref, *refs):
    values, scales = refs[:groups], refs[groups : 2 * groups]
    outs = refs[len(refs) - groups :]
    for value_ref, scale_ref, out_ref in zip(values, scales, outs):
        width = value_ref.shape[-2]
        latent_width = blocks * 128
        span = value_ref.shape[-1]
        factor = scale_ref[...].reshape(blocks, span).astype(jnp.float32)
        for block in range(blocks):
            rows = slice(block * 128, (block + 1) * 128)
            part = value_ref[..., rows, :].reshape(128, span).astype(jnp.float32)
            out_ref[0, rows, :] = (part * factor[block : block + 1, :]).astype(jnp.bfloat16)
        rest = value_ref[..., latent_width:width, :]
        out_ref[0, latent_width:width, :] = rest.reshape(width - latent_width, span)


def pack(values, scales, index, span, waits=()):
    groups, count = index.shape
    width, blocks = values.shape[-2], scales.shape[-2]

    def spec(rows, group):
        if values.ndim == 2:
            return pl.BlockSpec((rows, span), lambda n, index_ref: (0, index_ref[group, n]))
        return pl.BlockSpec((1, rows, span), lambda n, index_ref: (index_ref[group, n], 0, 0))

    return pl.pallas_call(
        lambda *refs: pack_kernel(groups, blocks, *refs),
        grid_spec=pltpu.PrefetchScalarGridSpec(
            num_scalar_prefetch=1,
            grid=(count,),
            in_specs=[spec(width, g) for g in range(groups)]
            + [spec(blocks, g) for g in range(groups)]
            + [pl.BlockSpec(memory_space=pl.ANY)] * len(waits),
            out_specs=[pl.BlockSpec((1, width, span), lambda n, index_ref: (n, 0, 0))] * groups,
        ),
        out_shape=[jax.ShapeDtypeStruct((count, width, span), jnp.bfloat16)] * groups,
        cost_estimate=SHORT,
    )(index, *([values] * groups), *([scales] * groups), *waits)


def pack_all(values, scales, index, span, *waits):
    groups, count = index.shape
    width, blocks = values.shape[-2], scales.shape[-2]

    def kernel(index_ref, *refs):
        outs = [refs[-1].at[g] for g in range(groups)]
        pack_kernel(groups, blocks, index_ref, *refs[: 2 * groups], *outs)

    def spec(rows, group):
        if values.ndim == 2:
            return pl.BlockSpec((rows, span), lambda n, index_ref: (0, index_ref[group, n]))
        return pl.BlockSpec((1, rows, span), lambda n, index_ref: (index_ref[group, n], 0, 0))

    return pl.pallas_call(
        kernel,
        grid_spec=pltpu.PrefetchScalarGridSpec(
            num_scalar_prefetch=1,
            grid=(count,),
            in_specs=[spec(width, g) for g in range(groups)]
            + [spec(blocks, g) for g in range(groups)]
            + [pl.BlockSpec(memory_space=pl.ANY)] * len(waits),
            out_specs=pl.BlockSpec(
                (groups, 1, width, span), lambda n, index_ref: (0, n, 0, 0)
            ),
        ),
        out_shape=jax.ShapeDtypeStruct((groups, count, width, span), jnp.bfloat16),
        cost_estimate=SHORT,
    )(index, *([values] * groups), *([scales] * groups), *waits)


def held(arrays, *waits):
    def kernel(*refs):
        pass

    anywhere = pl.BlockSpec(memory_space=pl.ANY)
    return pl.pallas_call(
        kernel,
        in_specs=[anywhere] * (len(arrays) + len(waits)),
        out_specs=[anywhere] * len(arrays),
        out_shape=[jax.ShapeDtypeStruct(x.shape, x.dtype) for x in arrays],
        input_output_aliases={i: i for i in range(len(arrays))},
        cost_estimate=SHORT,
    )(*arrays, *waits)


def regroup_kernel(count, *refs):
    refs = refs[: 2 * count] + refs[-2:]
    for k in range(count):
        refs[2 * count][k, 0] = refs[k][0]
        refs[2 * count + 1][k, 0] = refs[count + k][0]


def regroup(landed, *waits):
    count, (rows, width, span) = len(landed), landed[0].shape
    half = rows // 2
    own = pl.BlockSpec((1, width, span), lambda n: (n, 0, 0))
    far = pl.BlockSpec((1, width, span), lambda n: (half + n, 0, 0))
    outs = pl.pallas_call(
        lambda *refs: regroup_kernel(count, *refs),
        grid=(half,),
        in_specs=[own] * count
        + [far] * count
        + [pl.BlockSpec(memory_space=pl.ANY)] * len(waits),
        out_specs=[pl.BlockSpec((count, 1, width, span), lambda n: (0, n, 0, 0))] * 2,
        out_shape=[jax.ShapeDtypeStruct((count, half, width, span), jnp.bfloat16)] * 2,
        cost_estimate=SHORT,
    )(*landed, *landed, *waits)
    return tuple(x.reshape(count * half, width, span) for x in outs)


def regroup_arrived(arrived, offsets, me):
    rows, width, span = arrived.shape[1:]
    half, count = rows // 2, len(offsets)

    def spec(offset, first):
        return pl.BlockSpec(
            (1, 1, width, span), lambda n, me_ref: (me_ref[0] ^ offset, first + n, 0, 0)
        )

    def kernel(me_ref, *refs):
        for side in range(2):
            for k in range(count):
                refs[2 * count + side][k, 0] = refs[side * count + k][0, 0]

    outs = pl.pallas_call(
        kernel,
        grid_spec=pltpu.PrefetchScalarGridSpec(
            num_scalar_prefetch=1,
            grid=(half,),
            in_specs=[spec(k, 0) for k in offsets] + [spec(k, half) for k in offsets],
            out_specs=[pl.BlockSpec((count, 1, width, span), lambda n, me_ref: (0, n, 0, 0))] * 2,
        ),
        out_shape=[jax.ShapeDtypeStruct((count, half, width, span), jnp.bfloat16)] * 2,
        cost_estimate=SHORT,
    )(me[None], *([arrived] * (2 * count)))
    return tuple(x.reshape(count * half, width, span) for x in outs)


def select_kernel(sources, which_ref, index_ref, *refs):
    n = pl.program_id(0)
    refs = refs[: 2 * sources] + refs[-2:]
    for side in range(2):
        for source in range(sources):

            @pl.when(which_ref[side, n] == source)
            def _(side=side, source=source):
                refs[2 * sources + side][...] = refs[side * sources + source][...]


def select_blocks(arrived, which, index, *waits):
    count = index.shape[1]
    width, span = arrived[0].shape[1:]

    def pick(side, source):
        def place(n, which_ref, index_ref):
            return jnp.where(which_ref[side, n] == source, index_ref[side, n], 0), 0, 0

        return pl.BlockSpec((1, width, span), place)

    return pl.pallas_call(
        lambda *refs: select_kernel(len(arrived), *refs),
        grid_spec=pltpu.PrefetchScalarGridSpec(
            num_scalar_prefetch=2,
            grid=(count,),
            in_specs=[pick(i, j) for i in range(2) for j in range(len(arrived))]
            + [pl.BlockSpec(memory_space=pl.ANY)] * len(waits),
            out_specs=[pl.BlockSpec((1, width, span), lambda n, *refs: (n, 0, 0))] * 2,
        ),
        out_shape=[jax.ShapeDtypeStruct((count, width, span), jnp.bfloat16)] * 2,
        cost_estimate=SHORT,
    )(which, index, *arrived, *arrived, *waits)


def cut(wk, wv, pieces, which, *waits):
    width, narrow = wk.shape[1], wv.shape[1]
    rows, folds = wk.shape[0] // pieces, width // narrow

    def kernel(which_ref, wk_ref, wv_ref, *refs):
        refs[-1][:rows, :] = wk_ref[...]
        for fold in range(folds):
            columns = slice(fold * narrow, (fold + 1) * narrow)
            refs[-1][rows:, columns] = wv_ref[fold * rows : (fold + 1) * rows, :]

    def block(rows, columns):
        return pl.BlockSpec((rows, columns), lambda n, which_ref: (which_ref[0], 0))

    return pl.pallas_call(
        kernel,
        grid_spec=pltpu.PrefetchScalarGridSpec(
            num_scalar_prefetch=1,
            grid=(1,),
            in_specs=[block(rows, width), block(folds * rows, narrow)]
            + [pl.BlockSpec(memory_space=pl.ANY)] * len(waits),
            out_specs=pl.BlockSpec((2 * rows, width), lambda n, which_ref: (0, 0)),
        ),
        out_shape=jax.ShapeDtypeStruct((2 * rows, width), wk.dtype),
        cost_estimate=SHORT,
    )(which[None], wk, wv, *waits)


def doubled(near, far):
    count, rows, width = near.shape

    def kernel(near_ref, far_ref, out_ref):
        out_ref[0] = near_ref[...]
        out_ref[1] = far_ref[...]

    spec = pl.BlockSpec((1, rows, width), lambda n: (n, 0, 0))
    out = pl.pallas_call(
        kernel,
        grid=(count,),
        in_specs=[spec] * 2,
        out_specs=pl.BlockSpec((2, 1, rows, width), lambda n: (0, n, 0, 0)),
        out_shape=jax.ShapeDtypeStruct((2, count, rows, width), near.dtype),
        cost_estimate=SHORT,
    )(near, far)
    return out.reshape(2 * count, rows, width)


def in_order(near, far, replica, narrow, *waits):
    count, rows, width = near.shape
    rows, folds = rows // 2, width // narrow

    def pick(n, replica_ref):
        return (n ^ replica_ref[0]) // 2, 0, 0

    def kernel(replica_ref, near_ref, far_ref, *refs):
        wk_out, wv_out = refs[-2:]
        odd = (pl.program_id(0) ^ replica_ref[0]) & 1

        def put(source):
            wk_out[0] = source[0, :rows, :]
            for fold in range(folds):
                columns = slice(fold * narrow, (fold + 1) * narrow)
                wv_out[0, fold * rows : (fold + 1) * rows, :] = source[0, rows:, columns]

        @pl.when(odd == 0)
        def _():
            put(near_ref)

        @pl.when(odd == 1)
        def _():
            put(far_ref)

    return pl.pallas_call(
        kernel,
        grid_spec=pltpu.PrefetchScalarGridSpec(
            num_scalar_prefetch=1,
            grid=(2 * count,),
            in_specs=[pl.BlockSpec((1, 2 * rows, width), pick)] * 2
            + [pl.BlockSpec(memory_space=pl.ANY)] * len(waits),
            out_specs=[
                pl.BlockSpec((1, rows, width), lambda n, replica_ref: (n, 0, 0)),
                pl.BlockSpec((1, folds * rows, narrow), lambda n, replica_ref: (n, 0, 0)),
            ],
        ),
        out_shape=[
            jax.ShapeDtypeStruct((2 * count, rows, width), near.dtype),
            jax.ShapeDtypeStruct((2 * count, folds * rows, narrow), near.dtype),
        ],
        cost_estimate=SHORT,
    )(replica[None], near, far, *waits)


def by_side(arrays, index, *waits):
    count = index.shape[1]
    steps = arrays[0].shape[1]
    width = sum(x.shape[2] for x in arrays)

    def kernel(index_ref, *refs):
        outs, staged = refs[-3:-1], refs[-1]
        for side in range(2):
            first = 0
            for x_ref in refs[: len(arrays)]:
                columns = slice(first, first + x_ref.shape[2])
                first += x_ref.shape[2]
                for n in range(count):
                    rows = x_ref[index_ref[side, n]].astype(jnp.float32)
                    staged[n * steps : (n + 1) * steps, columns] = rows
            outs[side][...] = staged[...].astype(outs[side].dtype)

    vmem = pl.BlockSpec(memory_space=pltpu.VMEM)
    return pl.pallas_call(
        kernel,
        in_specs=[pl.BlockSpec(memory_space=pltpu.SMEM)]
        + [vmem] * len(arrays)
        + [pl.BlockSpec(memory_space=pl.ANY)] * len(waits),
        out_specs=[vmem] * 2,
        out_shape=[jax.ShapeDtypeStruct((count * steps, width), arrays[0].dtype)] * 2,
        scratch_shapes=[pltpu.VMEM((count * steps, width), jnp.float32)],
        compiler_params=pltpu.CompilerParams(vmem_limit_bytes=24 * 1024 * 1024),
        cost_estimate=SHORT,
    )(index, *arrays, *waits)


def absorb(queries, weights, steps, *waits):
    rows = queries.shape[0]
    heads, nope_width, latent_width = weights.shape
    rope_width = queries.shape[1] // heads - nope_width

    def kernel(queries_ref, weights_ref, *refs):
        latent_out, rope_out, latent_rows, rope_rows = refs[len(waits) :]
        for head in range(heads):
            place = pl.ds(head, rows, stride=heads)
            columns = slice(head * nope_width, (head + 1) * nope_width)
            product = jnp.dot(
                queries_ref[:, columns], weights_ref[head], preferred_element_type=jnp.float32
            )
            for block in range(latent_width // 128):
                latent_rows[block, place, :] = product[:, block * 128 : (block + 1) * 128]
            first = heads * nope_width + head * rope_width
            part = queries_ref[:, first : first + rope_width].astype(jnp.float32)
            rope_rows[place, :] = jnp.concatenate([part] * (128 // rope_width), axis=1)
        for block in range(latent_width // 128):
            columns = slice(block * 128, (block + 1) * 128)
            latent_out[:, columns] = latent_rows[block].astype(jnp.bfloat16)
        rope_out[...] = rope_rows[:, :rope_width].astype(jnp.bfloat16)

    vmem = pl.BlockSpec(memory_space=pltpu.VMEM)
    latent, rotary = pl.pallas_call(
        kernel,
        in_specs=[vmem] * 2 + [pl.BlockSpec(memory_space=pl.ANY)] * len(waits),
        out_specs=[vmem] * 2,
        out_shape=[
            jax.ShapeDtypeStruct((rows * heads, latent_width), jnp.bfloat16),
            jax.ShapeDtypeStruct((rows * heads, rope_width), jnp.bfloat16),
        ],
        scratch_shapes=[
            pltpu.VMEM((latent_width // 128, rows * heads, 128), jnp.float32),
            pltpu.VMEM((rows * heads, 128), jnp.float32),
        ],
        compiler_params=pltpu.CompilerParams(vmem_limit_bytes=24 * 1024 * 1024),
        cost_estimate=SHORT,
    )(queries, weights, *waits)
    slots = rows // steps
    return (
        latent.reshape(slots, steps * heads, latent_width),
        rotary.reshape(slots, steps * heads, rope_width),
    )


def attend_kernel(shards, steps, score_scale, scalars, *refs):
    queries = refs[:4]
    keys = refs[4 : 4 + shards]
    new_ref, own_out, other_out = refs[4 + shards], refs[-2], refs[-1]
    own_latent, other_latent, own_rope, other_rope = queries
    latent_width = own_latent.shape[2]
    span = keys[0].shape[2]
    length = scalars[1 + pl.program_id(0)]
    shard = scalars[0]
    key_columns = jnp.concatenate([ref[0] for ref in keys], axis=1)
    new_rows = new_ref[0]
    query = jnp.concatenate([own_latent[0], other_latent[0]], axis=0)
    rope = jnp.concatenate([own_rope[0], other_rope[0]], axis=0)
    across = (((1,), (1,)), ((), ()))
    along = (((1,), (0,)), ((), ()))

    def product(left, right, contract):
        return lax.dot_general(left, right, contract, preferred_element_type=jnp.float32)

    cache_scores = score_scale * (
        product(query, key_columns[:latent_width], along)
        + product(rope, key_columns[latent_width:], along)
    )
    new_scores = score_scale * (
        product(query, new_rows[:, :latent_width], across)
        + product(rope, new_rows[:, latent_width:], across)
    )
    column = lax.broadcasted_iota(jnp.int32, cache_scores.shape, 1)
    position = (shard ^ (column // span)) * span + column % span
    cache_live = position < length
    half = own_latent.shape[1]
    row = lax.broadcasted_iota(jnp.int32, new_scores.shape, 0)
    step = (row % half) // (half // steps)
    new_live = lax.broadcasted_iota(jnp.int32, new_scores.shape, 1) <= step
    cache_scores = jnp.where(cache_live, cache_scores, MASKED_SCORE)
    new_scores = jnp.where(new_live, new_scores, MASKED_SCORE)
    top = jnp.maximum(
        jnp.max(cache_scores, axis=1, keepdims=True), jnp.max(new_scores, axis=1, keepdims=True)
    )
    cache_weights = jnp.where(cache_live, jnp.exp(cache_scores - top), 0.0)
    new_weights = jnp.where(new_live, jnp.exp(new_scores - top), 0.0)
    weight_sum = jnp.sum(cache_weights, axis=1, keepdims=True) + jnp.sum(
        new_weights, axis=1, keepdims=True
    )
    mixed = product(
        cache_weights.astype(jnp.bfloat16), key_columns[:latent_width], across
    ) + product(new_weights.astype(jnp.bfloat16), new_rows[:, :latent_width], along)
    latent = (mixed / weight_sum).astype(jnp.bfloat16)
    own_out[0] = latent[:half]
    other_out[0] = latent[half:]


def attend(scalars, start, queries, keys, new_rows, steps, score_scale, waits):
    count, (half, latent_width) = keys[0].shape[0], queries[0].shape[1:]
    rope_width = queries[2].shape[2]
    width, span = keys[0].shape[1:]
    shards = len(keys)

    def block(rows, columns, first=0):
        return pl.BlockSpec((1, rows, columns), lambda n, scalars: (first + n, 0, 0))

    return pl.pallas_call(
        lambda *refs: attend_kernel(shards, steps, score_scale, *refs),
        grid_spec=pltpu.PrefetchScalarGridSpec(
            num_scalar_prefetch=1,
            grid=(count,),
            in_specs=[block(half, latent_width, start)] * 2
            + [block(half, rope_width, start)] * 2
            + [block(width, span)] * shards
            + [block(NEW_ROWS, width, start)]
            + [pl.BlockSpec(memory_space=pl.ANY)] * len(waits),
            out_specs=[block(half, latent_width)] * 2,
        ),
        out_shape=[jax.ShapeDtypeStruct((count, half, latent_width), jnp.bfloat16)] * 2,
        compiler_params=pltpu.CompilerParams(vmem_limit_bytes=32 * 1024 * 1024),
        cost_estimate=SHORT,
    )(scalars, *queries, *keys, new_rows, *waits)


def output(head_out, row_of, w_out, shards):
    rows, columns = row_of.shape[0], w_out.shape[1]
    depth, width = w_out.shape[0], 512
    while columns % width:
        width //= 2

    def kernel(row_ref, *refs):
        heads, w_ref = refs[: len(head_out)], refs[len(head_out)]
        outs, ordered = refs[len(head_out) + 1 : -1], refs[-1]

        @pl.when(pl.program_id(0) == 0)
        def _():
            place = lax.broadcasted_iota(jnp.int32, (rows, rows), 1)
            chosen = (place == row_ref[...]).astype(jnp.bfloat16)
            stacked = jnp.concatenate([ref[...] for ref in heads], axis=0)
            ordered[...] = jnp.dot(
                chosen, stacked, preferred_element_type=jnp.float32
            ).astype(jnp.bfloat16)

        result = jnp.dot(ordered[...], w_ref[...], preferred_element_type=jnp.float32)
        share = rows // shards
        for k in range(shards):
            outs[k][...] = result[k * share : (k + 1) * share].astype(jnp.bfloat16)

    def whole(x):
        return pl.BlockSpec(x.shape, lambda n: (0, 0))

    return pl.pallas_call(
        kernel,
        grid=(columns // width,),
        in_specs=[whole(row_of)]
        + [whole(x) for x in head_out]
        + [pl.BlockSpec((depth, width), lambda n: (0, n))],
        out_specs=[pl.BlockSpec((rows // shards, width), lambda n: (0, n))] * shards,
        out_shape=[jax.ShapeDtypeStruct((rows // shards, columns), jnp.bfloat16)] * shards,
        scratch_shapes=[pltpu.VMEM((rows, depth), jnp.bfloat16)],
        compiler_params=pltpu.CompilerParams(vmem_limit_bytes=30 * 1024 * 1024),
        cost_estimate=pl.CostEstimate(
            flops=2 * rows * depth * columns,
            bytes_accessed=2 * depth * columns,
            transcendentals=0,
        ),
    )(row_of, *head_out, w_out)


def local(kv_values, kv_scales, decode_of, kv_lengths, q_nope, q_rope, new_kv, wk_up, wv_up, w_out):
    groups = lax.axis_size("xfer")
    shards = lax.axis_size("tensor")
    me = lax.axis_index("xfer")
    shard = lax.axis_index("tensor")
    parity = shard % 2
    requests = decode_of.shape[0]
    per_group = requests // groups
    row_width = kv_values.shape[1]
    span = kv_values.shape[0] // per_group
    pair_share = per_group // groups
    pair_room = pair_share + pair_share // 2
    sure = pair_share - pair_share // 2
    late = pair_share // 2
    heads_here, nope_width, latent_width = wk_up.shape
    value_width = wv_up.shape[2]
    steps = q_nope.shape[1]
    rope_width = q_rope.shape[2] // heads_here
    score_scale = 1.0 / math.sqrt(nope_width + rope_width)
    out_rows = per_group // shards
    half = per_group // 2
    half_sure = sure // 2
    late_half = (per_group - groups * sure) // 4
    sizes = [2 * half_sure, (groups - 2) * half_sure, late_half, late_half]
    starts = [0, sizes[0], sizes[0] + sizes[1], sizes[0] + sizes[1] + sizes[2]]
    late_start = starts[2]

    def across(x, axis, offset, name="other"):
        with jax.named_scope(f"{name}_{axis if isinstance(axis, str) else 'both'}{offset}"):
            return lax.ppermute(x, axis, [(i, i ^ offset) for i in range(lax.axis_size(axis))])

    dest_here = lax.dynamic_slice_in_dim(decode_of, me * per_group, per_group)
    here = jnp.arange(per_group, dtype=jnp.int32)
    rank_here = jnp.sum(
        ((dest_here[:, None] == dest_here[None, :]) & (here[None, :] < here[:, None])).astype(
            jnp.int32
        ),
        axis=1,
    )
    place_here = dest_here * pair_room + rank_here
    early_ranks = jnp.arange(sure, dtype=jnp.int32)
    early_ranks = (early_ranks + parity * half_sure) % sure
    offsets = jnp.arange(groups, dtype=jnp.int32)
    early_places = (me ^ offsets)[:, None] * pair_room + early_ranks[None, :]
    late_ranks = jnp.arange(late, dtype=jnp.int32)
    middle_places = offsets[:, None] * pair_room + sure + late_ranks[None, :]
    last_places = middle_places + late

    def request_at(places):
        hit = places[..., None] == place_here
        return jnp.sum(jnp.where(hit, here, 0), axis=-1)

    if span % 128 == 0:
        values, scales = kv_values.T, kv_scales.T
    else:
        values = kv_values.reshape(per_group, span, -1).swapaxes(1, 2)
        scales = kv_scales.reshape(per_group, span, -1).swapaxes(1, 2)
    near = pack(values, scales, request_at(early_places[:2]), span)
    first = regroup([near[0], across(near[1], "xfer", 1, "early")])
    far_places = offsets[:, None] * pair_room + early_ranks[None, :]
    early_out = pack_all(values, scales, request_at(far_places), span, first[0])

    ids = jnp.arange(requests, dtype=jnp.int32)
    source = ids // per_group
    mine = decode_of == me
    before = ids[None, :] < ids[:, None]
    rank = jnp.sum(
        (
            before
            & (decode_of[None, :] == decode_of[:, None])
            & (source[None, :] == source[:, None])
        ).astype(jnp.int32),
        axis=1,
    )
    slot = jnp.sum((before & mine[None, :]).astype(jnp.int32), axis=1)
    is_late, is_last = rank >= sure, rank >= pair_share
    in_middle = mine & is_late & ~is_last
    late_rank = jnp.where(is_last, jnp.sum(in_middle.astype(jnp.int32)), 0) + jnp.sum(
        (before & ((mine & is_late)[None, :] & (is_last[None, :] == is_last[:, None]))).astype(
            jnp.int32
        ),
        axis=1,
    )
    offset = source ^ me
    first_place = offset * half_sure + rank % half_sure
    late_chunk, late_rest = late_rank // (2 * late_half), late_rank % (2 * late_half)
    late_place = late_start + late_chunk * late_half + late_rest % late_half
    side = jnp.where(is_late, late_rest // late_half, rank // half_sure) ^ parity
    place = side * half + jnp.where(is_late, late_place, first_place)
    hit = mine[None, :] & (place[None, :] == here[:, None])

    def at_place(values):
        return jnp.sum(jnp.where(hit, values[None, :], 0), axis=1)

    replicas = lax.axis_size("groups") * groups
    replica = lax.axis_index("groups") * groups + me
    slots = at_place(slot)
    lengths = at_place(kv_lengths)
    late_which = at_place(is_last.astype(jnp.int32)).reshape(2, half)[:, late_start:]
    late_index = at_place(source * late + (rank - sure) % late).reshape(2, half)[:, late_start:]
    place_of_slot = jnp.sum(
        jnp.where(mine[None, :] & (slot[None, :] == here[:, None]), place[None, :], 0), axis=1
    )

    def send_keys(chunk, name, waits=(), carried=()):
        if waits:
            own_keys, far_keys, *carried = held([*chunk, *carried], *waits)
        else:
            own_keys, far_keys = chunk
        keys = [own_keys] + [
            across(far_keys if k % 2 else own_keys, "tensor", k, name) for k in range(1, shards)
        ]
        return keys, *carried

    def land(out):
        return lax.all_to_all(out, "xfer", 0, 0, tiled=True)

    def flat(arrived):
        return arrived.reshape(groups * late, row_width, span)

    replicas = lax.axis_size("groups") * groups
    replica = lax.axis_index("groups") * groups + me

    def take(x, index):
        return jnp.take(x, index, axis=0, mode="clip")

    def attend_chunk(chunk, keys, waits):
        start = starts[chunk]
        live = lengths[start : start + sizes[chunk]]
        scalars = jnp.concatenate([shard[None], live]).astype(jnp.int32)
        queries = [latent_own, latent_far, rope_own, rope_far]
        return attend(scalars, start, queries, keys, new_own, steps, score_scale, waits)

    def project(latent, weights):
        size = latent.shape[0]
        out = jnp.einsum(
            "rthc,hcv->rthv",
            latent.reshape(size, steps, heads_here, latent_width),
            weights,
            preferred_element_type=jnp.float32,
        )
        return out.astype(jnp.bfloat16).reshape(size, steps, heads_here * value_width)

    wk, wv = (x.reshape(-1, x.shape[-1]) for x in (wk_up, wv_up))
    hops = [("xfer", 1 << i) for i in range(1, groups.bit_length() - 1)]
    hops += [("groups", 1 << i) for i in range((replicas // groups).bit_length() - 1)]
    keys = list(send_keys(first, "keys0"))
    stack = across(cut(wk, wv, replicas, replica, first[0]), "tensor", 1, "weights")[None]
    second = regroup_arrived(land(early_out), range(2, groups), me)
    sent, stack = send_keys(second, "keys1", keys[0][1:], [stack])
    keys.append(sent)
    queries_own, queries_far = by_side([q_nope, q_rope], slots.reshape(2, half), first[0])
    queries_far = across(queries_far, "tensor", 1, "queries")
    middle_out = pack_all(values, scales, request_at(middle_places), span, second[0])
    middle_in = flat(land(middle_out))
    last_out = pack_all(values, scales, request_at(last_places), span, *keys[0][1:])
    for axis, offset in hops[:-1]:
        stack = doubled(stack, across(stack, axis, offset, "weights"))
    third = select_blocks(
        [middle_in], jnp.zeros_like(late_which[:, :late_half]), late_index[:, :late_half]
    )
    latent_own, rope_own = absorb(queries_own, wk_up, steps, third[0])
    sent, stack = send_keys(third, "keys2", [*keys[1][1:], queries_far, latent_own, last_out], [stack])
    keys.append(sent)
    last_in = flat(land(last_out))
    for axis, offset in hops[-1:]:
        stack = doubled(stack, across(stack, axis, offset, "weights"))
    fourth = select_blocks(
        [middle_in, last_in], late_which[:, late_half:], late_index[:, late_half:]
    )
    sent, stack = send_keys(fourth, "keys3", keys[2][1:], [stack])
    keys.append(sent)
    wk_far, wv_far = in_order(stack, across(stack, "xfer", 1, "weights"), replica, wv.shape[-1])
    wk_far, wv_far = wk_far.reshape(wk_up.shape), wv_far.reshape(wv_up.shape)
    latent_far, rope_far = absorb(queries_far, wk_far, steps)
    new_own = take(new_kv, slots[:half])
    new_own = jnp.pad(new_own, ((0, 0), (0, NEW_ROWS - steps), (0, 0)))
    latents, own_heads, far_heads = [], [], []
    for chunk in range(4):
        waits = [x for x, _ in latents[-1:]] if chunk < 3 else own_heads + far_heads
        own, far = attend_chunk(chunk, keys[chunk], waits)
        latents.append((own, far))
        far_heads.append(project(far, wv_far))
        own_heads.append(project(own, wv_up))
    far_heads = [across(x, "tensor", 1, "heads") for x in far_heads]
    head_out = [x.reshape(-1, x.shape[-1]) for x in own_heads + far_heads]
    row = jnp.arange(per_group * steps, dtype=jnp.int32)
    slot_of_row = ((shard ^ (row // (out_rows * steps))) * out_rows * steps) + row % (
        out_rows * steps
    )
    row_of = jnp.take(place_of_slot, slot_of_row // steps, mode="clip") * steps + row % steps
    parts = output(head_out, row_of[:, None], w_out, shards)
    parts = [parts[0]] + [across(parts[k], "tensor", k, "output") for k in range(1, shards)]
    summed = sum(x.astype(jnp.float32) for x in parts).astype(jnp.bfloat16)
    return summed.reshape(out_rows, steps, -1)


def solution(mesh):
    return jax.shard_map(
        local,
        mesh=mesh,
        in_specs=(
            P(("groups", "xfer", "tensor"), None),
            P(("groups", "xfer", "tensor"), None),
            P("groups"),
            P("groups"),
            P(("groups", "xfer"), None, "tensor"),
            P(("groups", "xfer"), None, "tensor"),
            P(("groups", "xfer"), None, None),
            P("tensor", None, None),
            P("tensor", None, None),
            P("tensor", None),
        ),
        out_specs=P(("groups", "xfer", "tensor"), None, None),
        check_vma=False,
    )
```
